256 devices in a mesh: cp: 64 (over y, z, core), hp: 4 (over x).
Axes of the slice: x: 4, y: 4, z: 8, core: 2. Of those that a mesh axis runs over, the one named last changes fastest.
Arguments:
- query: bfloat16 [32768, 4096], P(('cp', 'hp')), may hold values from -6 to 6
- key: bfloat16 [32768, 512], P(('cp', 'hp')), may hold values from -6 to 6
- value: bfloat16 [32768, 512], P(('cp', 'hp')), may hold values from -6 to 6
- cotangent: bfloat16 [32768, 4096], P(('cp', 'hp')), may hold values from -6 to 6
- lengths: int32 [64], replicated, may hold values from 1 to 1536, 32768 in all
Outputs:
- attended: bfloat16 [32768, 4096], P(('cp', 'hp'))
- grad_query: bfloat16 [32768, 4096], P(('cp', 'hp'))
- grad_key: bfloat16 [32768, 512], P(('cp', 'hp'))
- grad_value: bfloat16 [32768, 512], P(('cp', 'hp'))
The draws below stay inside these ranges and needn't reach their ends.
Inputs may be any that keep to these rules, and one draw needn't show every extreme that they name: The lengths sum to 32768 and the largest is exactly 1536.
All inputs are finite; a program needn't handle non-finite values.
Results may differ from the reference program's by a relative error of at most 0.0087.
Values may be sent and summed in bfloat16 or wider, within the bound.
A program may use at most 128 MiB of HBM per device.

```python
import math
import jax
import jax.numpy as jnp
import numpy as np
from jax import lax

QUERY_HEADS = 32
KEY_VALUE_HEADS = 4
HEAD_DIMENSION = 128
SHARD_LOOKBACK = 3
SHARD_TOKENS = 512
MAXDOC = 1536
PACKED_TOKENS = 32768
NDOCS = 64
N_CP = 64


def draw_query(key, part):
    key = jax.random.fold_in(key, 1)
    group_ratio = QUERY_HEADS // KEY_VALUE_HEADS
    base_offset = jax.random.normal(key, (PACKED_TOKENS, KEY_VALUE_HEADS, group_ratio, HEAD_DIMENSION), jnp.float32)
    return jnp.clip(base_offset, -6.0, 6.0).reshape(PACKED_TOKENS, QUERY_HEADS * HEAD_DIMENSION).astype(jnp.bfloat16)


def draw_key(key, part):
    key = jax.random.fold_in(key, 2)
    base_offset = jax.random.normal(key, (PACKED_TOKENS, KEY_VALUE_HEADS, HEAD_DIMENSION), jnp.float32)
    return jnp.clip(base_offset, -6.0, 6.0).reshape(PACKED_TOKENS, KEY_VALUE_HEADS * HEAD_DIMENSION).astype(jnp.bfloat16)


def block_scale(own_key, extent, cuts, smallest, high):
    def one(position, shards_of):
        heights = jax.random.uniform(jax.random.fold_in(jax.random.fold_in(own_key, 6), position), (shards_of,), jnp.float32, smallest / len(cuts), high / len(cuts))
        return jnp.repeat(jnp.exp(heights), extent[position] // shards_of).reshape((-1,) + (1,) * (len(extent) - position - 1))

    loudness = one(*cuts[0])
    for cut in cuts[1:]:
        loudness = loudness * one(*cut)
    return loudness


def length_profile(amount, total, most, skew):
    loads = [(1 << 20) // math.isqrt(standing ** skew) + 1 for standing in range(2, amount + 1)]
    rest, holding = total - most - (amount - 1), [1] * (amount - 1)
    while rest > 0:
        movable = [i for i in range(amount - 1) if holding[i] < most]
        whole, left = sum([loads[i] for i in movable]), rest
        for i in movable:
            more = min(most - holding[i], max(1, left * loads[i] // whole), rest)
            holding[i] = holding[i] + more
            rest = rest - more
    return np.array([most] + holding)


def uneven(rng, number_of, total, most, lean):
    if number_of == 2:
        one = jax.random.randint(rng, (), max(1, total - most), min(most, total - 1) + 1)
        return jnp.stack([one, total - one])
    sizes = jnp.asarray(length_profile(number_of, total, most, lean), jnp.int32)
    pairs = (number_of - 1) // 2
    source_of, taker = sizes[1:1 + 2 * pairs:2], sizes[2:2 + 2 * pairs:2]
    slack = jnp.minimum(source_of - 1, most - taker)
    passed = jax.random.randint(jax.random.fold_in(rng, 1), (pairs,), 0, 1 << 20) % (slack + 1)
    sizes = sizes.at[1:1 + 2 * pairs:2].set(source_of - passed).at[2:2 + 2 * pairs:2].set(taker + passed)
    return sizes[jax.random.permutation(jax.random.fold_in(rng, 2), number_of)]


def centred(key, extent, spread, most, cuts=(), kind=jnp.bfloat16):
    level = block_scale(key, extent, cuts, -0.22, 0.18) if cuts else 1.0
    drawn = jax.random.normal(key, extent, jnp.float32) * spread * level
    return jnp.minimum(jnp.maximum(drawn, -most), most).astype(kind)


def setup_inputs(seed: int = 0) -> dict:
    arg_keys = jax.random.split(jax.random.key(seed), 6)
    return {
        "query": draw_query(jax.random.fold_in(arg_keys[5], 71), 0),
        "key": draw_key(jax.random.fold_in(arg_keys[5], 71), 0),
        "value": centred(arg_keys[2], (PACKED_TOKENS, KEY_VALUE_HEADS * HEAD_DIMENSION), 1.0, 6.0, ((0, 256),)),
        "cotangent": centred(arg_keys[3], (PACKED_TOKENS, QUERY_HEADS * HEAD_DIMENSION), 1.0, 6.0, ((0, 256),)),
        "lengths": uneven(arg_keys[4], NDOCS, PACKED_TOKENS, MAXDOC, 2).astype(jnp.int32),
    }


def document_ids(lengths, positions):
    ends = jnp.cumsum(lengths).astype(jnp.int32)
    counted = jnp.sum((ends[None, :] <= positions[:, None]).astype(jnp.int32), axis=1).astype(jnp.int32)
    return jnp.where(positions >= 0, counted, -1).astype(jnp.int32)


def rounded(values):
    return lax.optimization_barrier(values.astype(jnp.bfloat16)).astype(jnp.float32)


def reference(query, key, value, cotangent, lengths):
    group_ratio = QUERY_HEADS // KEY_VALUE_HEADS
    window_span = (SHARD_LOOKBACK + 1) * SHARD_TOKENS
    scaling = HEAD_DIMENSION ** -0.5
    front_portion = jnp.zeros((SHARD_LOOKBACK * SHARD_TOKENS, KEY_VALUE_HEADS * HEAD_DIMENSION), key.dtype)
    padded_keys = jnp.concatenate([front_portion, key], axis=0)
    padded_values = jnp.concatenate([front_portion, value], axis=0)
    zero_gradient = jnp.zeros((PACKED_TOKENS + SHARD_LOOKBACK * SHARD_TOKENS, KEY_VALUE_HEADS * HEAD_DIMENSION), jnp.float32)

    def one_block(sums, index):
        grad_keys, grad_values = sums
        first_index = (index * SHARD_TOKENS).astype(jnp.int32)
        query_block = lax.dynamic_slice_in_dim(query, first_index, SHARD_TOKENS, 0).astype(jnp.float32).reshape(SHARD_TOKENS, KEY_VALUE_HEADS, group_ratio, HEAD_DIMENSION)
        gradient_block = lax.dynamic_slice_in_dim(cotangent, first_index, SHARD_TOKENS, 0).astype(jnp.float32).reshape(SHARD_TOKENS, KEY_VALUE_HEADS, group_ratio, HEAD_DIMENSION)
        key_window = lax.dynamic_slice_in_dim(padded_keys, first_index, window_span, 0).astype(jnp.float32).reshape(window_span, KEY_VALUE_HEADS, HEAD_DIMENSION)
        value_window = lax.dynamic_slice_in_dim(padded_values, first_index, window_span, 0).astype(jnp.float32).reshape(window_span, KEY_VALUE_HEADS, HEAD_DIMENSION)
        query_pos = first_index + jnp.arange(SHARD_TOKENS, dtype=jnp.int32)
        key_pos = first_index - SHARD_LOOKBACK * SHARD_TOKENS + jnp.arange(window_span, dtype=jnp.int32)
        allowed = (document_ids(lengths, query_pos)[:, None] == document_ids(lengths, key_pos)[None, :]) & (key_pos[None, :] <= query_pos[:, None])
        scores = jnp.einsum("sgpd,kgd->gpsk", query_block, key_window) * scaling
        scores = jnp.where(allowed, scores, -jnp.inf)
        largest = jnp.max(scores, axis=-1, keepdims=True)
        log_total = largest + jnp.log(jnp.sum(jnp.exp(scores - largest), axis=-1, keepdims=True))
        weights = jnp.exp(scores - log_total)
        weight_matrix_second = rounded(weights)
        output = jnp.einsum("gpsk,kgd->sgpd", weight_matrix_second, value_window)
        delta = jnp.sum(gradient_block * output, axis=-1).transpose(1, 2, 0)[..., None]
        grad_w = jnp.einsum("sgpd,kgd->gpsk", gradient_block, value_window)
        score_gradient = rounded(weights * (grad_w - delta) * scaling)
        grad_q = jnp.einsum("gpsk,kgd->sgpd", score_gradient, key_window)
        key_portion = jnp.einsum("lyte,tlyz->elz", score_gradient, query_block).reshape(window_span, KEY_VALUE_HEADS * HEAD_DIMENSION)
        value_portion = jnp.einsum("lyte,tlyz->elz", weight_matrix_second, gradient_block).reshape(window_span, KEY_VALUE_HEADS * HEAD_DIMENSION)
        grad_keys = lax.dynamic_update_slice_in_dim(grad_keys, lax.dynamic_slice_in_dim(grad_keys, first_index, window_span, 0) + key_portion, first_index, 0)
        grad_values = lax.dynamic_update_slice_in_dim(grad_values, lax.dynamic_slice_in_dim(grad_values, first_index, window_span, 0) + value_portion, first_index, 0)
        outputs = (output.reshape(SHARD_TOKENS, QUERY_HEADS * HEAD_DIMENSION).astype(jnp.bfloat16), grad_q.reshape(SHARD_TOKENS, QUERY_HEADS * HEAD_DIMENSION).astype(jnp.bfloat16))
        return (grad_keys, grad_values), outputs

    sums, stacked = lax.scan(one_block, (zero_gradient, zero_gradient), jnp.arange(N_CP, dtype=jnp.int32))
    attended = stacked[0].reshape(PACKED_TOKENS, QUERY_HEADS * HEAD_DIMENSION)
    grad_query = stacked[1].reshape(PACKED_TOKENS, QUERY_HEADS * HEAD_DIMENSION)
    grad_key = sums[0][SHARD_LOOKBACK * SHARD_TOKENS:].astype(jnp.bfloat16)
    grad_value = sums[1][SHARD_LOOKBACK * SHARD_TOKENS:].astype(jnp.bfloat16)
    return (attended, grad_query, grad_key, grad_value)
```

```python
import functools
import math

import jax
import jax.numpy as jnp
from jax import lax
from jax.experimental import pallas as pl
from jax.experimental.pallas import tpu as pltpu
from jax.sharding import PartitionSpec as P

HEAD = 128
REACH = 3
TILE = 256
TILES = 7
CHUNK_HEADS = 2
OUTSIDE = -16384.0
NT = (((1,), (1,)), ((), ()))
TN = (((0,), (0,)), ((), ()))
NN = (((1,), (0,)), ((), ()))
F32 = jnp.float32
BF16 = jnp.bfloat16
MESH = pl.DeviceIdType.MESH


def dot(a, b, dims):
    return lax.dot_general(a, b, dims, preferred_element_type=F32)


def kernel(
    cp_size, hp_size, tokens, heads,
    query, key, value, cotangent, lens,
    attended, grad_query, grad_key, grad_value,
    qb, db, kx, vx, qe, s0, s1, pb, dsb, ob, dqb, acc, inv, dox, qn, don, akk, avv, sendb, recvb, gb,
    kv_send, kv_recv, win_send, win_recv, q_send, q_recv, d_send, d_recv,
    o_send, o_recv, dq_send, dq_recv, part_send, part_recv, g_send, g_recv, local,
):
    shard = tokens * hp_size
    pairs = shard // TILE
    window = (REACH + 1) * shard
    chunks = heads // CHUNK_HEADS
    rows = TILE * CHUNK_HEADS
    wide = CHUNK_HEADS * HEAD
    group = heads * HEAD
    place = lax.axis_index("cp")
    me = lax.axis_index("hp")
    scale = HEAD ** -0.5
    to_log2 = scale * math.log2(math.e)
    others = range(1, hp_size)
    mine = pl.ds(pl.multiple_of(me * tokens, tokens), tokens)

    def hp_peer(step):
        return lax.rem(me + step, hp_size)

    def cp_peer(step):
        return lax.rem(place + step + cp_size, cp_size)

    barrier = pltpu.get_barrier_semaphore()
    for step in others:
        pl.semaphore_signal(barrier, 1, device_id=(place, hp_peer(step)), device_id_type=MESH)
    for step in range(1, REACH + 1):
        pl.semaphore_signal(barrier, 1, device_id=(cp_peer(step), me), device_id_type=MESH)
        pl.semaphore_signal(barrier, 1, device_id=(cp_peer(-step), me), device_id_type=MESH)
    pl.semaphore_wait(barrier, hp_size - 1 + 2 * REACH)

    def columns(start, width):
        return pl.ds(pl.multiple_of(start, HEAD), width)

    def kv_copy(which, step):
        source, landing = ((key, kx), (value, vx))[which]
        to = hp_peer(step)
        return pltpu.make_async_remote_copy(
            src_ref=source.at[:, columns(to * HEAD, HEAD)],
            dst_ref=landing.at[pl.ds(pl.multiple_of(REACH * shard + me * tokens, tokens), tokens), pl.ds(0, HEAD)],
            send_sem=kv_send.at[which, step - 1], recv_sem=kv_recv.at[which, step - 1],
            device_id=(place, to), device_id_type=MESH)

    def in_copy(which, chunk, step):
        source, landing, send, recv = ((query, qb, q_send, q_recv), (cotangent, db, d_send, d_recv))[which]
        to = hp_peer(step)
        return pltpu.make_async_remote_copy(
            src_ref=source.at[:, columns(to * group + chunk * wide, wide)],
            dst_ref=landing.at[mine, columns(chunk * wide, wide)],
            send_sem=send.at[chunk, step - 1], recv_sem=recv.at[chunk, step - 1],
            device_id=(place, to), device_id_type=MESH)

    def out_copy(which, chunk, step):
        source, landing, send, recv = ((ob, attended, o_send, o_recv), (dqb, grad_query, dq_send, dq_recv))[which]
        to = hp_peer(step)
        return pltpu.make_async_remote_copy(
            src_ref=source.at[pl.ds(pl.multiple_of(to * tokens, tokens), tokens), columns(chunk * wide, wide)],
            dst_ref=landing.at[:, columns(me * group + chunk * wide, wide)],
            send_sem=send.at[chunk, step - 1], recv_sem=recv.at[chunk, step - 1],
            device_id=(place, to), device_id_type=MESH)

    def window_copy(which, step):
        ref = (kx, vx)[which]
        return pltpu.make_async_remote_copy(
            src_ref=ref.at[pl.ds(REACH * shard, shard), pl.ds(0, HEAD)],
            dst_ref=ref.at[pl.ds((REACH - step) * shard, shard), pl.ds(0, HEAD)],
            send_sem=win_send.at[which, step - 1], recv_sem=win_recv.at[which, step - 1],
            device_id=(cp_peer(step), me), device_id_type=MESH)

    def part_copy(block):
        return pltpu.make_async_remote_copy(
            src_ref=sendb.at[block], dst_ref=recvb.at[block],
            send_sem=part_send.at[block], recv_sem=part_recv.at[block],
            device_id=(cp_peer(block - REACH), me), device_id_type=MESH)

    def grad_copy(which, step):
        to = hp_peer(step)
        return pltpu.make_async_remote_copy(
            src_ref=gb.at[which, pl.ds(pl.multiple_of(to * tokens, tokens), tokens), :],
            dst_ref=(grad_key, grad_value)[which].at[:, columns(me * HEAD, HEAD)],
            send_sem=g_send.at[which, step - 1], recv_sem=g_recv.at[which, step - 1],
            device_id=(place, to), device_id_type=MESH)

    own = [
        pltpu.make_async_copy(
            source.at[:, columns(me * HEAD, HEAD)],
            landing.at[pl.ds(pl.multiple_of(REACH * shard + me * tokens, tokens), tokens), pl.ds(0, HEAD)],
            local.at[number])
        for number, (source, landing) in enumerate(((key, kx), (value, vx)))
    ] + [
        pltpu.make_async_copy(source.at[:, columns(me * group, group)], landing.at[mine, :], local.at[2 + number])
        for number, (source, landing) in enumerate(((query, qb), (cotangent, db)))
    ]
    for which in range(2):
        for step in others:
            kv_copy(which, step).start()
    for copy in own:
        copy.start()

    def start_in(which):
        def body(chunk, carry):
            for step in others:
                in_copy(which, chunk, step).start()
            return carry
        lax.fori_loop(0, chunks, body, 0)

    start_in(0)
    start_in(1)

    documents = lens.shape[0]
    lower = lax.broadcasted_iota(jnp.int32, (documents, HEAD), 0)
    upper = lax.broadcasted_iota(jnp.int32, (documents, HEAD), 1)
    counts = jnp.broadcast_to(lens[...], (documents, HEAD)).astype(F32)
    ends = jnp.sum(jnp.where(lower <= upper, counts, 0.0), axis=0, keepdims=True)
    starts = jnp.sum(jnp.where(lower < upper, counts, 0.0), axis=0, keepdims=True)
    number = lax.broadcasted_iota(jnp.int32, (1, HEAD), 1)
    ends = jnp.where(number == documents, 0.0, ends).astype(jnp.int32)
    starts = jnp.where(number == documents, -1e6, starts).astype(jnp.int32)

    def inside(first, amount):
        at = lax.broadcasted_iota(jnp.int32, (amount, HEAD), 0) + first
        return (at >= starts) & (at < ends)

    qe[...] = jnp.where(inside(place * shard, shard), 0.0, OUTSIDE).astype(BF16)
    kx[:, HEAD:] = jnp.where(inside((place - REACH) * shard, window), 1.0, 0.0).astype(BF16)
    vx[:, HEAD:] = jnp.ones((window, HEAD), BF16)

    for which in range(2):
        own[which].wait()
        for step in others:
            kv_copy(which, step).wait_recv()
        for step in range(1, REACH + 1):
            window_copy(which, step).start()
    own[2].wait()
    for step in range(1, REACH + 1):
        window_copy(0, step).wait_recv()

    def wait_in(which, chunk):
        for step in others:
            in_copy(which, chunk, step).wait_recv()

    def stacked(ref, chunk, pair):
        block = ref[pair * TILE:(pair + 1) * TILE, columns(chunk * wide, wide)]
        return jnp.concatenate([block[:, head * HEAD:(head + 1) * HEAD] for head in range(CHUNK_HEADS)], axis=0)

    def unstacked(block):
        return jnp.concatenate([block[head * TILE:(head + 1) * TILE] for head in range(CHUNK_HEADS)], axis=1)

    def chunk_rows(chunk):
        return pl.ds(pl.multiple_of(chunk * rows, rows), rows)

    scores = (s0, s1)
    at_row = lax.broadcasted_iota(jnp.int32, (rows, TILE), 0) % TILE
    at_column = lax.broadcasted_iota(jnp.int32, (rows, TILE), 1)
    lane = lax.broadcasted_iota(jnp.int32, (rows, HEAD), 1)

    def forward(later, now):
        if later is not None:
            chunk, pair = later
            extra = qe[pair * TILE:(pair + 1) * TILE, :]
            qx = jnp.concatenate([stacked(qb, chunk, pair), jnp.concatenate([extra] * CHUNK_HEADS, axis=0)], axis=1)
        if now is not None:
            chunk_now, pair_now = now
            at = chunk_rows(chunk_now)
            top = s1 if pair_now else s0
            highest = top[:, TILES * TILE:]
        running = None
        for tile in range(TILES):
            span = slice(tile * TILE, (tile + 1) * TILE)
            if later is not None:
                s = dot(qx, kx[pair * TILE + tile * TILE:pair * TILE + (tile + 1) * TILE, :], NT)
                if tile == TILES - 1:
                    s = jnp.where(at_column <= at_row, s, OUTSIDE)
                scores[pair][:, span] = s
                half = jnp.maximum(s[:, :HEAD], s[:, HEAD:])
                running = half if running is None else jnp.maximum(running, half)
            if now is not None:
                shifted = scores[pair_now][:, span] * to_log2 - jnp.concatenate([highest, highest], axis=1)
                pb[tile, pair_now, at, :] = jnp.exp2(shifted).astype(BF16)
        if later is not None:
            most = jnp.max(running, axis=1, keepdims=True) * to_log2
            scores[pair][:, TILES * TILE:] = jnp.broadcast_to(most, (rows, HEAD))
        if now is not None:
            total = None
            for tile in range(TILES):
                first = pair_now * TILE + tile * TILE
                part = dot(pb[tile, pair_now, at, :], vx[first:first + TILE, :], NN)
                total = part if total is None else total + part
            reciprocal = 1.0 / total[:, HEAD:]
            out = total[:, :HEAD] * reciprocal
            inv[pair_now, at, :] = reciprocal
            acc[pair_now, at, :] = out
            ob[pair_now * TILE:(pair_now + 1) * TILE, columns(chunk_now * wide, wide)] = unstacked(out.astype(BF16))

    def send_out(which, chunk):
        for step in others:
            out_copy(which, chunk, step).start()

    wait_in(0, 0)
    forward((0, 0), None)
    for step in range(1, REACH + 1):
        window_copy(1, step).wait_recv()

    def forward_step(chunk, carry):
        forward((chunk, 1), (chunk, 0))
        wait_in(0, chunk + 1)
        forward((chunk + 1, 0), (chunk, 1))
        send_out(0, chunk)
        return carry

    lax.fori_loop(0, chunks - 1, forward_step, 0)
    forward((chunks - 1, 1), (chunks - 1, 0))
    forward(None, (chunks - 1, 1))
    send_out(0, chunks - 1)
    own_out = pltpu.make_async_copy(ob.at[mine, :], attended.at[:, columns(me * group, group)], local.at[4])
    own_out.start()

    own[3].wait()

    def prepare(chunk, carry):
        wait_in(1, chunk)
        at = chunk_rows(chunk)
        for pair in range(pairs):
            given = stacked(db, chunk, pair)
            wide_given = given.astype(F32)
            out = acc[pair, at, :]
            reciprocal = inv[pair, at, :]
            delta = -jnp.sum(wide_given * out, axis=1, keepdims=True)
            high = delta.astype(BF16).astype(F32)
            rest = delta - high
            middle = rest.astype(BF16).astype(F32)
            low = rest - middle
            extra = jnp.where(lane == 0, high, jnp.where(lane == 1, middle, jnp.where(lane == 2, low, 0.0)))
            dox[pair, at, :HEAD] = given
            dox[pair, at, HEAD:] = extra.astype(BF16)
            don[pair, at, :] = (wide_given * reciprocal).astype(BF16)
            qn[pair, at, :] = (stacked(qb, chunk, pair).astype(F32) * (reciprocal * scale)).astype(BF16)
            acc[pair, at, :] = jnp.zeros((rows, HEAD), F32)
        return carry

    lax.fori_loop(0, chunks, prepare, 0)

    def tile_rows(tile):
        return pl.ds(pl.multiple_of(tile * TILE, TILE), TILE)

    def one_chunk(tile, pair, at):
        weights = pb[tile - pair, pair, at, :]
        dweight = dot(dox[pair, at, :], vx[tile_rows(tile), :], NT)
        ds = (weights.astype(F32) * dweight).astype(BF16)
        dsb[pair, at, :] = ds
        acc[pair, at, :] += dot(ds, kx[tile_rows(tile), pl.ds(0, HEAD)], NN)

    def whole_tile(tile, which):
        dk = dv = None
        for pair in which:
            for chunk in range(chunks):
                one_chunk(tile, pair, slice(chunk * rows, (chunk + 1) * rows))
        for pair in which:
            more_k = dot(dsb[pair], qn[pair], TN)
            more_v = dot(pb[tile - pair, pair], don[pair], TN)
            dk = more_k if dk is None else dk + more_k
            dv = more_v if dv is None else dv + more_v
        return dk, dv

    far = shard // TILE

    def store_part(tile, gradients):
        block = tile // far
        at = pl.ds(pl.multiple_of((tile % far) * TILE, TILE), TILE)
        sendb[block, at, :HEAD] = gradients[0].astype(BF16)
        sendb[block, at, HEAD:] = gradients[1].astype(BF16)

    store_part(0, whole_tile(0, (0,)))
    store_part(1, whole_tile(1, (0, 1)))
    part_copy(0).start()

    def backward_step(block, carry):
        store_part(block * far, whole_tile(block * far, (0, 1)))
        store_part(block * far + 1, whole_tile(block * far + 1, (0, 1)))
        part_copy(block).start()
        return carry

    lax.fori_loop(1, REACH, backward_step, 0)

    akk[...] = jnp.zeros_like(akk)
    avv[...] = jnp.zeros_like(avv)
    last = REACH * far

    def last_step(chunk, carry):
        at = chunk_rows(chunk)
        for tile, pair in ((last, 0), (last, 1), (last + 1, 1)):
            one_chunk(tile, pair, at)
            span = slice((tile - last) * TILE, (tile - last + 1) * TILE)
            akk[span, :] += dot(dsb[pair, at, :], qn[pair, at, :], TN)
            avv[span, :] += dot(pb[tile - pair, pair, at, :], don[pair, at, :], TN)
        for pair in range(pairs):
            gradient = acc[pair, at, :] * (inv[pair, at, :] * scale)
            dqb[pair * TILE:(pair + 1) * TILE, columns(chunk * wide, wide)] = unstacked(gradient.astype(BF16))
        send_out(1, chunk)
        return carry

    lax.fori_loop(0, chunks, last_step, 0)
    own_dq = pltpu.make_async_copy(dqb.at[mine, :], grad_query.at[:, columns(me * group, group)], local.at[5])
    own_dq.start()

    for block in range(REACH):
        part_copy(block).wait_recv()
    for which, total in enumerate((akk, avv)):
        span = slice(which * HEAD, (which + 1) * HEAD)
        whole = total[...]
        for block in range(REACH):
            whole = whole + recvb[block, :, span].astype(F32)
        gb[which] = whole.astype(BF16)
    own_g = [
        pltpu.make_async_copy(gb.at[which, mine, :], ref.at[:, columns(me * HEAD, HEAD)], local.at[6 + which])
        for which, ref in enumerate((grad_key, grad_value))
    ]
    for which in range(2):
        for step in others:
            grad_copy(which, step).start()
        own_g[which].start()

    for which in range(2):
        for step in others:
            kv_copy(which, step).wait_send()
        for step in range(1, REACH + 1):
            window_copy(which, step).wait_send()
    for block in range(REACH):
        part_copy(block).wait_send()

    def drain(chunk, carry):
        for step in others:
            in_copy(0, chunk, step).wait_send()
            in_copy(1, chunk, step).wait_send()
            out_copy(0, chunk, step).wait()
            out_copy(1, chunk, step).wait()
        return carry

    lax.fori_loop(0, chunks, drain, 0)
    own_out.wait()
    own_dq.wait()
    for which in range(2):
        own_g[which].wait()
        for step in others:
            grad_copy(which, step).wait()


def per_device(query, key, value, cotangent, lengths):
    cp_size = lax.axis_size("cp")
    hp_size = lax.axis_size("hp")
    tokens = query.shape[0]
    heads = query.shape[1] // (HEAD * hp_size)
    shard = tokens * hp_size
    pairs = shard // TILE
    window = (REACH + 1) * shard
    chunks = heads // CHUNK_HEADS
    rows = TILE * CHUNK_HEADS
    total = heads * TILE
    anywhere = pl.BlockSpec(memory_space=pl.ANY)
    vmem = pltpu.VMEM
    dma = pltpu.SemaphoreType.DMA
    peers = hp_size - 1
    scratch = [
        vmem((shard, heads * HEAD), BF16),
        vmem((shard, heads * HEAD), BF16),
        vmem((window, 2 * HEAD), BF16),
        vmem((window, 2 * HEAD), BF16),
        vmem((shard, HEAD), BF16),
        vmem((rows, TILES * TILE + HEAD), F32),
        vmem((rows, TILES * TILE + HEAD), F32),
        vmem((TILES, pairs, total, TILE), BF16),
        vmem((pairs, total, TILE), BF16),
        vmem((shard, heads * HEAD), BF16),
        vmem((shard, heads * HEAD), BF16),
        vmem((pairs, total, HEAD), F32),
        vmem((pairs, total, HEAD), F32),
        vmem((pairs, total, 2 * HEAD), BF16),
        vmem((pairs, total, HEAD), BF16),
        vmem((pairs, total, HEAD), BF16),
        vmem((shard, HEAD), F32),
        vmem((shard, HEAD), F32),
        vmem((REACH, shard, 2 * HEAD), BF16),
        vmem((REACH, shard, 2 * HEAD), BF16),
        vmem((2, shard, HEAD), BF16),
        dma((2, peers)), dma((2, peers)),
        dma((2, REACH)), dma((2, REACH)),
        dma((chunks, peers)), dma((chunks, peers)),
        dma((chunks, peers)), dma((chunks, peers)),
        dma((chunks, peers)), dma((chunks, peers)),
        dma((chunks, peers)), dma((chunks, peers)),
        dma((REACH,)), dma((REACH,)),
        dma((2, peers)), dma((2, peers)),
        dma((8,)),
    ]
    shape = jax.ShapeDtypeStruct
    return pl.pallas_call(
        functools.partial(kernel, cp_size, hp_size, tokens, heads),
        out_shape=(
            shape(query.shape, BF16),
            shape(query.shape, BF16),
            shape(key.shape, BF16),
            shape(value.shape, BF16),
        ),
        in_specs=[anywhere] * 4 + [pl.BlockSpec(memory_space=pltpu.VMEM)],
        out_specs=[anywhere] * 4,
        scratch_shapes=scratch,
        compiler_params=pltpu.CompilerParams(
            collective_id=0, has_side_effects=True, vmem_limit_bytes=56 << 20
        ),
    )(query, key, value, cotangent, lengths.reshape(-1, 1))


def solution(mesh):
    spec = P(("cp", "hp"), None)
    return jax.shard_map(
        per_device,
        mesh=mesh,
        in_specs=(spec, spec, spec, spec, P()),
        out_specs=(spec, spec, spec, spec),
        check_vma=False,
    )
```

```python
import functools
import math

import jax
import jax.numpy as jnp
from jax import lax
from jax.experimental import pallas as pl
from jax.experimental.pallas import tpu as pltpu
from jax.sharding import PartitionSpec as P

HEAD = 128
REACH = 3
TILE = 256
TILES = 7
CHUNK_HEADS = 2
OUTSIDE = -16384.0
AT_ONCE = 4
NT = (((1,), (1,)), ((), ()))
NN = (((1,), (0,)), ((), ()))
F32 = jnp.float32
BF16 = jnp.bfloat16
MESH = pl.DeviceIdType.MESH


def dot(a, b, dims):
    return lax.dot_general(a, b, dims, preferred_element_type=F32)


def kernel(
    cp_size, hp_size, tokens, heads,
    query, key, value, cotangent, lengths,
    attended, grad_query, grad_key, grad_value,
    lens, qb, db, kx, vx, qe, pb, dsb, ob, dqb, acc, total, top, tops, dox, dt, qt, akk, avv, sendb, recvb, gb,
    kv_send, kv_recv, win_send, win_recv, q_send, q_recv, d_send, d_recv,
    o_send, o_recv, dq_send, dq_recv, part_send, part_recv, g_send, g_recv, local,
):
    shard = tokens * hp_size
    pairs = shard // TILE
    window = (REACH + 1) * shard
    chunks = heads // CHUNK_HEADS
    rows = TILE * CHUNK_HEADS
    wide = CHUNK_HEADS * HEAD
    group = heads * HEAD
    place = lax.axis_index("cp")
    me = lax.axis_index("hp")
    scale = HEAD ** -0.5
    to_log2 = scale * math.log2(math.e)
    others = range(1, hp_size)
    mine = pl.ds(pl.multiple_of(me * tokens, tokens), tokens)

    def hp_peer(step):
        return lax.rem(me + step, hp_size)

    def cp_peer(step):
        return lax.rem(place + step + cp_size, cp_size)

    barrier = pltpu.get_barrier_semaphore()
    for step in others:
        pl.semaphore_signal(barrier, 1, device_id=(place, hp_peer(step)), device_id_type=MESH)
    for step in range(1, REACH + 1):
        pl.semaphore_signal(barrier, 1, device_id=(cp_peer(step), me), device_id_type=MESH)
        pl.semaphore_signal(barrier, 1, device_id=(cp_peer(-step), me), device_id_type=MESH)
    pl.semaphore_wait(barrier, hp_size - 1 + 2 * REACH)

    def columns(start, width):
        return pl.ds(pl.multiple_of(start, HEAD), width)

    def kv_copy(which, step):
        source, landing = ((key, kx), (value, vx))[which]
        to = hp_peer(step)
        return pltpu.make_async_remote_copy(
            src_ref=source.at[:, columns(to * HEAD, HEAD)],
            dst_ref=landing.at[pl.ds(pl.multiple_of(REACH * shard + me * tokens, tokens), tokens), pl.ds(0, HEAD)],
            send_sem=kv_send.at[which, step - 1], recv_sem=kv_recv.at[which, step - 1],
            device_id=(place, to), device_id_type=MESH)

    def in_copy(which, chunk, step):
        source, landing, send, recv = ((query, qb, q_send, q_recv), (cotangent, db, d_send, d_recv))[which]
        to = hp_peer(step)
        return pltpu.make_async_remote_copy(
            src_ref=source.at[:, columns(to * group + chunk * wide, wide)],
            dst_ref=landing.at[mine, columns(chunk * wide, wide)],
            send_sem=send.at[chunk, step - 1], recv_sem=recv.at[chunk, step - 1],
            device_id=(place, to), device_id_type=MESH)

    def out_copy(which, chunk, step):
        source, landing, send, recv = ((ob, attended, o_send, o_recv), (dqb, grad_query, dq_send, dq_recv))[which]
        to = hp_peer(step)
        return pltpu.make_async_remote_copy(
            src_ref=source.at[pl.ds(pl.multiple_of(to * tokens, tokens), tokens), columns(chunk * wide, wide)],
            dst_ref=landing.at[:, columns(me * group + chunk * wide, wide)],
            send_sem=send.at[chunk, step - 1], recv_sem=recv.at[chunk, step - 1],
            device_id=(place, to), device_id_type=MESH)

    def window_copy(which, step):
        ref = (kx, vx)[which]
        return pltpu.make_async_remote_copy(
            src_ref=ref.at[pl.ds(REACH * shard, shard), pl.ds(0, HEAD)],
            dst_ref=ref.at[pl.ds((REACH - step) * shard, shard), pl.ds(0, HEAD)],
            send_sem=win_send.at[which, step - 1], recv_sem=win_recv.at[which, step - 1],
            device_id=(cp_peer(step), me), device_id_type=MESH)

    def part_copy(block):
        return pltpu.make_async_remote_copy(
            src_ref=sendb.at[block], dst_ref=recvb.at[block],
            send_sem=part_send.at[block], recv_sem=part_recv.at[block],
            device_id=(cp_peer(block - REACH), me), device_id_type=MESH)

    def grad_copy(which, step):
        to = hp_peer(step)
        return pltpu.make_async_remote_copy(
            src_ref=gb.at[which, pl.ds(pl.multiple_of(to * tokens, tokens), tokens), :],
            dst_ref=(grad_key, grad_value)[which].at[:, columns(me * HEAD, HEAD)],
            send_sem=g_send.at[which, step - 1], recv_sem=g_recv.at[which, step - 1],
            device_id=(place, to), device_id_type=MESH)

    own_lens = pltpu.make_async_copy(lengths, lens, local.at[8])
    own = [
        pltpu.make_async_copy(
            source.at[:, columns(me * HEAD, HEAD)],
            landing.at[pl.ds(pl.multiple_of(REACH * shard + me * tokens, tokens), tokens), pl.ds(0, HEAD)],
            local.at[number])
        for number, (source, landing) in enumerate(((key, kx), (value, vx)))
    ] + [
        pltpu.make_async_copy(source.at[:, columns(me * group, group)], landing.at[mine, :], local.at[2 + number])
        for number, (source, landing) in enumerate(((query, qb), (cotangent, db)))
    ]
    for which in range(2):
        for step in others:
            kv_copy(which, step).start()
    own_lens.start()
    for copy in own:
        copy.start()

    def start_in(which):
        def body(chunk, carry):
            for step in others:
                in_copy(which, chunk, step).start()
            return carry
        lax.fori_loop(0, chunks, body, 0)

    start_in(0)
    start_in(1)

    documents = lens.shape[1]
    lower = lax.broadcasted_iota(jnp.int32, (documents, HEAD), 0)
    upper = lax.broadcasted_iota(jnp.int32, (documents, HEAD), 1)
    own_lens.wait()
    counts = jnp.broadcast_to(lens[...], (8, documents))
    coarse = (counts // 256).astype(BF16)
    fine = (counts % 256).astype(BF16)

    def added(mask):
        taken = jnp.where(mask, 1.0, 0.0).astype(BF16)
        return (256.0 * dot(coarse, taken, NN) + dot(fine, taken, NN))[:1]

    number = lax.broadcasted_iota(jnp.int32, (1, HEAD), 1)
    ends = jnp.where(number == documents, 0.0, added(lower <= upper)).astype(jnp.int32)
    starts = jnp.where(number == documents, -1e6, added(lower < upper)).astype(jnp.int32)

    def inside(first, amount):
        at = lax.broadcasted_iota(jnp.int32, (amount, HEAD), 0) + first
        return (at >= starts) & (at < ends)

    qe[...] = jnp.where(inside(place * shard, shard), 0.0, OUTSIDE).astype(BF16)
    kx[:, HEAD:] = jnp.where(inside((place - REACH) * shard, window), 1.0, 0.0).astype(BF16)
    vx[:, HEAD:] = jnp.ones((window, HEAD), BF16)

    for which in range(2):
        own[which].wait()
        for step in others:
            kv_copy(which, step).wait_recv()
        window_copy(which, 1).start()
    for step in range(2, REACH + 1):
        for which in range(2):
            window_copy(which, step).start()
    own[2].wait()

    def wait_in(which, chunk):
        for step in others:
            in_copy(which, chunk, step).wait_recv()

    def stacked(ref, chunk, pair):
        block = ref[pair * TILE:(pair + 1) * TILE, columns(chunk * wide, wide)]
        return jnp.concatenate([block[:, head * HEAD:(head + 1) * HEAD] for head in range(CHUNK_HEADS)], axis=0)

    def unstacked(block):
        return jnp.concatenate([block[head * TILE:(head + 1) * TILE] for head in range(CHUNK_HEADS)], axis=1)

    def chunk_rows(chunk):
        return pl.ds(pl.multiple_of(chunk * rows, rows), rows)

    far = shard // TILE
    last = REACH * far
    at_row = lax.broadcasted_iota(jnp.int32, (rows, TILE), 0) % TILE
    at_column = lax.broadcasted_iota(jnp.int32, (rows, TILE), 1)
    lane = lax.broadcasted_iota(jnp.int32, (rows, HEAD), 1)

    def twice(block):
        return jnp.concatenate([block, block], axis=1)

    def tiles_of(step, pair):
        first = (REACH - step) * far
        return [tile for tile in range(first, first + far) if pair <= tile < pair + TILES]

    def look(step, chunk, pair):
        extra = qe[pair * TILE:(pair + 1) * TILE, :]
        qx = jnp.concatenate([stacked(qb, chunk, pair), jnp.concatenate([extra] * CHUNK_HEADS, axis=0)], axis=1)
        running = None
        found = []
        for tile in tiles_of(step, pair):
            s = dot(qx, kx[tile * TILE:(tile + 1) * TILE, :], NT) * to_log2
            if tile == last + pair:
                s = jnp.where(at_column <= at_row, s, OUTSIDE)
            found.append(s)
            half = jnp.maximum(s[:, :HEAD], s[:, HEAD:])
            running = half if running is None else jnp.maximum(running, half)
        return found, running

    def attend(step, chunk, pair, found, running):
        at = chunk_rows(chunk)
        most = jnp.broadcast_to(jnp.max(running, axis=1, keepdims=True), (rows, HEAD))
        tops[step, pair, at, :] = most
        part = None
        for tile, s in zip(tiles_of(step, pair), found):
            weights = jnp.exp2(s - twice(most)).astype(BF16)
            pb[tile - pair, pair, at, :] = weights
            more = dot(weights, vx[tile * TILE:(tile + 1) * TILE, :], NN)
            part = more if part is None else part + more
        if step == 0:
            acc[pair, at, :] = part[:, :HEAD]
            total[pair, at, :] = part[:, HEAD:]
            top[pair, at, :] = most
        else:
            before = top[pair, at, :]
            highest = jnp.maximum(before, most)
            old = jnp.exp2(before - highest)
            new = jnp.exp2(most - highest)
            out = acc[pair, at, :] * old + part[:, :HEAD] * new
            weight = total[pair, at, :] * old + part[:, HEAD:] * new
            if step < REACH:
                acc[pair, at, :] = out
                total[pair, at, :] = weight
                top[pair, at, :] = highest
            else:
                out = out / weight
                acc[pair, at, :] = out
                top[pair, at, :] = highest + jnp.log2(weight)
                ob[pair * TILE:(pair + 1) * TILE, columns(chunk * wide, wide)] = unstacked(out.astype(BF16))

    def forward(step, chunk):
        work = [(chunk + more, pair) for more in range(AT_ONCE) for pair in range(pairs)]
        ahead = [look(step, *work[0])]
        for number, piece in enumerate(work):
            if number + 1 < len(work):
                ahead.append(look(step, *work[number + 1]))
            attend(step, *piece, *ahead[number])

    def send_out(which, chunk):
        for step in others:
            out_copy(which, chunk, step).start()

    for step in range(REACH + 1):
        if step:
            window_copy(0, step).wait_recv()
            window_copy(1, step).wait_recv()

        def forward_step(number, carry, step=step):
            chunk = number * AT_ONCE
            for more in range(AT_ONCE):
                if step == 0:
                    wait_in(0, chunk + more)
            forward(step, chunk)
            for more in range(AT_ONCE):
                if step == REACH:
                    send_out(0, chunk + more)
            return carry

        lax.fori_loop(0, chunks // AT_ONCE, forward_step, 0)
    own_out = pltpu.make_async_copy(ob.at[mine, :], attended.at[:, columns(me * group, group)], local.at[4])
    own_out.start()

    own[3].wait()

    def prepare(chunk, carry):
        wait_in(1, chunk)
        at = chunk_rows(chunk)
        for pair in range(pairs):
            given = stacked(db, chunk, pair)
            wide_given = given.astype(F32)
            out = acc[pair, at, :]
            delta = -jnp.sum(wide_given * out, axis=1, keepdims=True)
            high = delta.astype(BF16).astype(F32)
            rest = delta - high
            middle = rest.astype(BF16).astype(F32)
            low = rest - middle
            extra = jnp.where(lane == 0, high, jnp.where(lane == 1, middle, jnp.where(lane == 2, low, 0.0)))
            dox[pair, at, :HEAD] = given
            dox[pair, at, HEAD:] = extra.astype(BF16)
            dt[pair, :, at] = wide_given.T.astype(BF16)
            qt[pair, :, at] = stacked(qb, chunk, pair).astype(F32).T.astype(BF16)
            acc[pair, at, :] = jnp.zeros((rows, HEAD), F32)
        return carry

    lax.fori_loop(0, chunks, prepare, 0)

    def tile_rows(tile):
        return pl.ds(pl.multiple_of(tile * TILE, TILE), TILE)

    def one_chunk(tile, pair, at):
        factor = jnp.exp2(tops[REACH - tile // far, pair, at, :] - top[pair, at, :])
        weights = pb[tile - pair, pair, at, :].astype(F32) * twice(factor)
        pb[tile - pair, pair, at, :] = weights.astype(BF16)
        dweight = dot(dox[pair, at, :], vx[tile_rows(tile), :], NT)
        ds = (weights * dweight).astype(BF16)
        dsb[pair, at, :] = ds
        acc[pair, at, :] += dot(ds, kx[tile_rows(tile), pl.ds(0, HEAD)], NN)

    def whole_tile(tile, which):
        dk = dv = None
        for pair in which:
            for chunk in range(chunks):
                one_chunk(tile, pair, slice(chunk * rows, (chunk + 1) * rows))
        for pair in which:
            more_k = dot(qt[pair], dsb[pair], NN)
            more_v = dot(dt[pair], pb[tile - pair, pair], NN)
            dk = more_k if dk is None else dk + more_k
            dv = more_v if dv is None else dv + more_v
        return dk, dv

    def store_part(tile, gradients):
        block = tile // far
        at = pl.ds(pl.multiple_of((tile % far) * TILE, TILE), TILE)
        sendb[block, at, :HEAD] = (gradients[0] * scale).T.astype(BF16)
        sendb[block, at, HEAD:] = gradients[1].T.astype(BF16)

    store_part(0, whole_tile(0, (0,)))
    store_part(1, whole_tile(1, (0, 1)))
    part_copy(0).start()

    def backward_step(block, carry):
        store_part(block * far, whole_tile(block * far, (0, 1)))
        store_part(block * far + 1, whole_tile(block * far + 1, (0, 1)))
        part_copy(block).start()
        return carry

    lax.fori_loop(1, REACH, backward_step, 0)

    akk[...] = jnp.zeros_like(akk)
    avv[...] = jnp.zeros_like(avv)
    def last_step(chunk, carry):
        at = chunk_rows(chunk)
        for tile, pair in ((last, 0), (last, 1), (last + 1, 1)):
            one_chunk(tile, pair, at)
            span = slice((tile - last) * TILE, (tile - last + 1) * TILE)
            akk[:, span] += dot(qt[pair, :, at], dsb[pair, at, :], NN)
            avv[:, span] += dot(dt[pair, :, at], pb[tile - pair, pair, at, :], NN)
        for pair in range(pairs):
            gradient = acc[pair, at, :] * scale
            dqb[pair * TILE:(pair + 1) * TILE, columns(chunk * wide, wide)] = unstacked(gradient.astype(BF16))
        send_out(1, chunk)
        return carry

    lax.fori_loop(0, chunks, last_step, 0)
    own_dq = pltpu.make_async_copy(dqb.at[mine, :], grad_query.at[:, columns(me * group, group)], local.at[5])
    own_dq.start()

    for block in range(REACH):
        part_copy(block).wait_recv()
    for which, added_up in enumerate((akk, avv)):
        span = slice(which * HEAD, (which + 1) * HEAD)
        whole = (added_up[...] if which else added_up[...] * scale).T
        for block in range(REACH):
            whole = whole + recvb[block, :, span].astype(F32)
        gb[which] = whole.astype(BF16)
    own_g = [
        pltpu.make_async_copy(gb.at[which, mine, :], ref.at[:, columns(me * HEAD, HEAD)], local.at[6 + which])
        for which, ref in enumerate((grad_key, grad_value))
    ]
    for which in range(2):
        for step in others:
            grad_copy(which, step).start()
        own_g[which].start()

    for which in range(2):
        for step in others:
            kv_copy(which, step).wait_send()
        for step in range(1, REACH + 1):
            window_copy(which, step).wait_send()
    for block in range(REACH):
        part_copy(block).wait_send()

    def drain(chunk, carry):
        for step in others:
            in_copy(0, chunk, step).wait_send()
            in_copy(1, chunk, step).wait_send()
            out_copy(0, chunk, step).wait()
            out_copy(1, chunk, step).wait()
        return carry

    lax.fori_loop(0, chunks, drain, 0)
    own_out.wait()
    own_dq.wait()
    for which in range(2):
        own_g[which].wait()
        for step in others:
            grad_copy(which, step).wait()


def per_device(query, key, value, cotangent, lengths):
    cp_size = lax.axis_size("cp")
    hp_size = lax.axis_size("hp")
    tokens = query.shape[0]
    heads = query.shape[1] // (HEAD * hp_size)
    shard = tokens * hp_size
    pairs = shard // TILE
    window = (REACH + 1) * shard
    chunks = heads // CHUNK_HEADS
    rows = TILE * CHUNK_HEADS
    total = heads * TILE
    anywhere = pl.BlockSpec(memory_space=pl.ANY)
    vmem = pltpu.VMEM
    dma = pltpu.SemaphoreType.DMA
    peers = hp_size - 1
    documents = lengths.shape[0]
    scratch = [
        vmem((1, documents), jnp.int32),
        vmem((shard, heads * HEAD), BF16),
        vmem((shard, heads * HEAD), BF16),
        vmem((window, 2 * HEAD), BF16),
        vmem((window, 2 * HEAD), BF16),
        vmem((shard, HEAD), BF16),
        vmem((TILES, pairs, total, TILE), BF16),
        vmem((pairs, total, TILE), BF16),
        vmem((shard, heads * HEAD), BF16),
        vmem((shard, heads * HEAD), BF16),
        vmem((pairs, total, HEAD), F32),
        vmem((pairs, total, HEAD), F32),
        vmem((pairs, total, HEAD), F32),
        vmem((REACH + 1, pairs, total, HEAD), F32),
        vmem((pairs, total, 2 * HEAD), BF16),
        vmem((pairs, HEAD, total), BF16),
        vmem((pairs, HEAD, total), BF16),
        vmem((HEAD, shard), F32),
        vmem((HEAD, shard), F32),
        vmem((REACH, shard, 2 * HEAD), BF16),
        vmem((REACH, shard, 2 * HEAD), BF16),
        vmem((2, shard, HEAD), BF16),
        dma((2, peers)), dma((2, peers)),
        dma((2, REACH)), dma((2, REACH)),
        dma((chunks, peers)), dma((chunks, peers)),
        dma((chunks, peers)), dma((chunks, peers)),
        dma((chunks, peers)), dma((chunks, peers)),
        dma((chunks, peers)), dma((chunks, peers)),
        dma((REACH,)), dma((REACH,)),
        dma((2, peers)), dma((2, peers)),
        dma((9,)),
    ]
    return pl.pallas_call(
        functools.partial(kernel, cp_size, hp_size, tokens, heads),
        out_shape=tuple(vmem(array.shape, BF16) for array in (query, query, key, value)),
        in_specs=[anywhere] * 5,
        out_specs=[pl.BlockSpec(memory_space=vmem)] * 4,
        scratch_shapes=scratch,
        compiler_params=pltpu.CompilerParams(
            collective_id=0, has_side_effects=True, vmem_limit_bytes=56 << 20
        ),
    )(query, key, value, cotangent, lengths.reshape(1, -1))


def solution(mesh):
    spec = P(("cp", "hp"), None)
    return jax.shard_map(
        per_device,
        mesh=mesh,
        in_specs=(spec, spec, spec, spec, P()),
        out_specs=(spec, spec, spec, spec),
        check_vma=False,
    )
```

```python
import functools
import math

import jax
import jax.numpy as jnp
from jax import lax
from jax.experimental import pallas as pl
from jax.experimental.pallas import tpu as pltpu
from jax.sharding import PartitionSpec as P

HEAD = 128
REACH = 3
TILE = 256
TILES = 7
CHUNK_HEADS = 2
OUTSIDE = -16384.0
AT_ONCE = 4
SLOTS = 4
NT = (((1,), (1,)), ((), ()))
NN = (((1,), (0,)), ((), ()))
F32 = jnp.float32
BF16 = jnp.bfloat16
MESH = pl.DeviceIdType.MESH


def dot(a, b, dims):
    return lax.dot_general(a, b, dims, preferred_element_type=F32)


def kernel(
    cp_size, hp_size, tokens, heads,
    query, key, value, cotangent, lengths,
    attended, grad_query, grad_key, grad_value,
    lens, qb, db, kx, vx, qe, pb, dsb, ob, dqb, acc, total, top, tops, dox, dt, qt, akk, avv, sendb, recvb, gb,
    kv_send, kv_recv, win_send, win_recv, q_send, q_recv, d_send, d_recv,
    o_send, o_recv, dq_send, dq_recv, part_send, part_recv, g_send, g_recv, local,
):
    shard = tokens * hp_size
    pairs = shard // TILE
    window = (REACH + 1) * shard
    chunks = heads // CHUNK_HEADS
    rows = TILE * CHUNK_HEADS
    wide = CHUNK_HEADS * HEAD
    group = heads * HEAD
    place = lax.axis_index("cp")
    me = lax.axis_index("hp")
    scale = HEAD ** -0.5
    to_log2 = scale * math.log2(math.e)
    others = range(1, hp_size)
    mine = pl.ds(pl.multiple_of(me * tokens, tokens), tokens)

    def hp_peer(step):
        return lax.rem(me + step, hp_size)

    def cp_peer(step):
        return lax.rem(place + step + cp_size, cp_size)

    barrier = pltpu.get_barrier_semaphore()
    for step in others:
        pl.semaphore_signal(barrier, 1, device_id=(place, hp_peer(step)), device_id_type=MESH)
    for step in range(1, REACH + 1):
        pl.semaphore_signal(barrier, 1, device_id=(cp_peer(step), me), device_id_type=MESH)
        pl.semaphore_signal(barrier, 1, device_id=(cp_peer(-step), me), device_id_type=MESH)
    pl.semaphore_wait(barrier, hp_size - 1 + 2 * REACH)

    def columns(start, width):
        return pl.ds(pl.multiple_of(start, HEAD), width)

    def kv_copy(which, step):
        source, landing = ((key, kx), (value, vx))[which]
        to = hp_peer(step)
        return pltpu.make_async_remote_copy(
            src_ref=source.at[:, columns(to * HEAD, HEAD)],
            dst_ref=landing.at[pl.ds(pl.multiple_of(REACH * shard + me * tokens, tokens), tokens), pl.ds(0, HEAD)],
            send_sem=kv_send.at[which, step - 1], recv_sem=kv_recv.at[which, step - 1],
            device_id=(place, to), device_id_type=MESH)

    def in_copy(which, chunk, step):
        source, landing, send, recv = ((query, qb, q_send, q_recv), (cotangent, db, d_send, d_recv))[which]
        to = hp_peer(step)
        return pltpu.make_async_remote_copy(
            src_ref=source.at[:, columns(to * group + chunk * wide, wide)],
            dst_ref=landing.at[mine, columns(chunk * wide, wide)],
            send_sem=send.at[chunk, step - 1], recv_sem=recv.at[chunk, step - 1],
            device_id=(place, to), device_id_type=MESH)

    def out_copy(which, chunk, step):
        source, landing, send, recv = ((ob, attended, o_send, o_recv), (dqb, grad_query, dq_send, dq_recv))[which]
        to = hp_peer(step)
        return pltpu.make_async_remote_copy(
            src_ref=source.at[pl.ds(pl.multiple_of(to * tokens, tokens), tokens), columns(chunk * wide, wide)],
            dst_ref=landing.at[:, columns(me * group + chunk * wide, wide)],
            send_sem=send.at[chunk, step - 1], recv_sem=recv.at[chunk, step - 1],
            device_id=(place, to), device_id_type=MESH)

    def window_copy(which, step):
        ref = (kx, vx)[which]
        return pltpu.make_async_remote_copy(
            src_ref=ref.at[pl.ds(REACH * shard, shard), pl.ds(0, HEAD)],
            dst_ref=ref.at[pl.ds((REACH - step) * shard, shard), pl.ds(0, HEAD)],
            send_sem=win_send.at[which, step - 1], recv_sem=win_recv.at[which, step - 1],
            device_id=(cp_peer(step), me), device_id_type=MESH)

    def part_copy(block):
        return pltpu.make_async_remote_copy(
            src_ref=sendb.at[block], dst_ref=recvb.at[block],
            send_sem=part_send.at[block], recv_sem=part_recv.at[block],
            device_id=(cp_peer(block - REACH), me), device_id_type=MESH)

    def grad_copy(which, step):
        to = hp_peer(step)
        return pltpu.make_async_remote_copy(
            src_ref=gb.at[which, pl.ds(pl.multiple_of(to * tokens, tokens), tokens), :],
            dst_ref=(grad_key, grad_value)[which].at[:, columns(me * HEAD, HEAD)],
            send_sem=g_send.at[which, step - 1], recv_sem=g_recv.at[which, step - 1],
            device_id=(place, to), device_id_type=MESH)

    own_lens = pltpu.make_async_copy(lengths, lens, local.at[8])
    own = [
        pltpu.make_async_copy(
            source.at[:, columns(me * HEAD, HEAD)],
            landing.at[pl.ds(pl.multiple_of(REACH * shard + me * tokens, tokens), tokens), pl.ds(0, HEAD)],
            local.at[number])
        for number, (source, landing) in enumerate(((key, kx), (value, vx)))
    ] + [
        pltpu.make_async_copy(source.at[:, columns(me * group, group)], landing.at[mine, :], local.at[2 + number])
        for number, (source, landing) in enumerate(((query, qb), (cotangent, db)))
    ]
    for which in range(2):
        for step in others:
            kv_copy(which, step).start()
    own_lens.start()
    for copy in own:
        copy.start()

    def start_in(which):
        def body(chunk, carry):
            for step in others:
                in_copy(which, chunk, step).start()
            return carry
        lax.fori_loop(0, chunks, body, 0)

    start_in(0)
    start_in(1)

    documents = lens.shape[1]
    lower = lax.broadcasted_iota(jnp.int32, (documents, HEAD), 0)
    upper = lax.broadcasted_iota(jnp.int32, (documents, HEAD), 1)
    own_lens.wait()
    counts = jnp.broadcast_to(lens[...], (8, documents))
    coarse = (counts // 256).astype(BF16)
    fine = (counts % 256).astype(BF16)

    def added(mask):
        taken = jnp.where(mask, 1.0, 0.0).astype(BF16)
        return (256.0 * dot(coarse, taken, NN) + dot(fine, taken, NN))[:1]

    number = lax.broadcasted_iota(jnp.int32, (1, HEAD), 1)
    ends = jnp.where(number == documents, 0.0, added(lower <= upper)).astype(jnp.int32)
    starts = jnp.where(number == documents, -1e6, added(lower < upper)).astype(jnp.int32)

    def inside(first, amount):
        at = lax.broadcasted_iota(jnp.int32, (amount, HEAD), 0) + first
        return (at >= starts) & (at < ends)

    qe[...] = jnp.where(inside(place * shard, shard), 0.0, OUTSIDE).astype(BF16)
    kx[:, HEAD:] = jnp.where(inside((place - REACH) * shard, window), 1.0, 0.0).astype(BF16)
    vx[:, HEAD:] = jnp.ones((window, HEAD), BF16)

    for which in range(2):
        own[which].wait()
        for step in others:
            kv_copy(which, step).wait_recv()
        window_copy(which, 1).start()
    for step in range(2, REACH + 1):
        for which in range(2):
            window_copy(which, step).start()
    own[2].wait()

    def wait_in(which, chunk):
        for step in others:
            in_copy(which, chunk, step).wait_recv()

    def stacked(ref, chunk, pair):
        block = ref[pair * TILE:(pair + 1) * TILE, columns(chunk * wide, wide)]
        return jnp.concatenate([block[:, head * HEAD:(head + 1) * HEAD] for head in range(CHUNK_HEADS)], axis=0)

    def unstacked(block):
        return jnp.concatenate([block[head * TILE:(head + 1) * TILE] for head in range(CHUNK_HEADS)], axis=1)

    def chunk_rows(chunk):
        return pl.ds(pl.multiple_of(chunk * rows, rows), rows)

    far = shard // TILE
    last = REACH * far
    at_row = lax.broadcasted_iota(jnp.int32, (rows, TILE), 0) % TILE
    at_column = lax.broadcasted_iota(jnp.int32, (rows, TILE), 1)
    lane = lax.broadcasted_iota(jnp.int32, (rows, HEAD), 1)

    def twice(block):
        return jnp.concatenate([block, block], axis=1)

    def tiles_of(step, pair):
        first = (REACH - step) * far
        return [tile for tile in range(first, first + far) if pair <= tile < pair + TILES]

    def look(step, chunk, pair):
        extra = qe[pair * TILE:(pair + 1) * TILE, :]
        qx = jnp.concatenate([stacked(qb, chunk, pair), jnp.concatenate([extra] * CHUNK_HEADS, axis=0)], axis=1)
        running = None
        found = []
        for tile in tiles_of(step, pair):
            s = dot(qx, kx[tile * TILE:(tile + 1) * TILE, :], NT) * to_log2
            if tile == last + pair:
                s = jnp.where(at_column <= at_row, s, OUTSIDE)
            found.append(s)
            half = jnp.maximum(s[:, :HEAD], s[:, HEAD:])
            running = half if running is None else jnp.maximum(running, half)
        return found, running

    def attend(step, chunk, pair, found, running):
        at = chunk_rows(chunk)
        most = jnp.broadcast_to(jnp.max(running, axis=1, keepdims=True), (rows, HEAD))
        tops[step, pair, at, :] = most
        part = None
        for tile, s in zip(tiles_of(step, pair), found):
            weights = jnp.exp2(s - twice(most)).astype(BF16)
            pb[tile - pair, pair, at, :] = weights
            more = dot(weights, vx[tile * TILE:(tile + 1) * TILE, :], NN)
            part = more if part is None else part + more
        if step == 0:
            acc[pair, at, :] = part[:, :HEAD]
            total[pair, at, :] = part[:, HEAD:]
            top[pair, at, :] = most
        else:
            before = top[pair, at, :]
            highest = jnp.maximum(before, most)
            old = jnp.exp2(before - highest)
            new = jnp.exp2(most - highest)
            out = acc[pair, at, :] * old + part[:, :HEAD] * new
            weight = total[pair, at, :] * old + part[:, HEAD:] * new
            if step < REACH:
                acc[pair, at, :] = out
                total[pair, at, :] = weight
                top[pair, at, :] = highest
            else:
                out = out / weight
                acc[pair, at, :] = out
                top[pair, at, :] = highest + jnp.log2(weight)
                ob[pair * TILE:(pair + 1) * TILE, columns(chunk * wide, wide)] = unstacked(out.astype(BF16))

    def forward(step, chunk):
        work = [(chunk + more, pair) for more in range(AT_ONCE) for pair in range(pairs)]
        ahead = [look(step, *work[0])]
        for number, piece in enumerate(work):
            if number + 1 < len(work):
                ahead.append(look(step, *work[number + 1]))
            attend(step, *piece, *ahead[number])

    def send_out(which, chunk):
        for step in others:
            out_copy(which, chunk, step).start()

    def turn_queries(chunk, carry):
        for pair in range(pairs):
            qt[pair, :, chunk_rows(chunk)] = stacked(qb, chunk, pair).astype(F32).T.astype(BF16)
        return carry

    for step in range(REACH + 1):
        if step == 1:
            lax.fori_loop(0, chunks, turn_queries, 0)
        if step:
            window_copy(0, step).wait_recv()
            window_copy(1, step).wait_recv()

        def forward_step(number, carry, step=step):
            chunk = number * AT_ONCE
            for more in range(AT_ONCE):
                if step == 0:
                    wait_in(0, chunk + more)
            forward(step, chunk)
            for more in range(AT_ONCE):
                if step == REACH:
                    send_out(0, chunk + more)
            return carry

        lax.fori_loop(0, chunks // AT_ONCE, forward_step, 0)
    own_out = pltpu.make_async_copy(ob.at[mine, :], attended.at[:, columns(me * group, group)], local.at[4])
    own_out.start()

    own[3].wait()

    def prepare(chunk, carry):
        wait_in(1, chunk)
        at = chunk_rows(chunk)
        for pair in range(pairs):
            given = stacked(db, chunk, pair)
            wide_given = given.astype(F32)
            out = acc[pair, at, :]
            delta = -jnp.sum(wide_given * out, axis=1, keepdims=True)
            high = delta.astype(BF16).astype(F32)
            rest = delta - high
            middle = rest.astype(BF16).astype(F32)
            low = rest - middle
            extra = jnp.where(lane == 0, high, jnp.where(lane == 1, middle, jnp.where(lane == 2, low, 0.0)))
            dox[pair, at, :HEAD] = given
            dox[pair, at, HEAD:] = extra.astype(BF16)
            dt[pair, :, at] = wide_given.T.astype(BF16)
            acc[pair, at, :] = jnp.zeros((rows, HEAD), F32)
        return carry

    lax.fori_loop(0, chunks, prepare, 0)

    def score_gradient(tile, pair, at):
        factor = jnp.exp2(tops[REACH - tile // far, pair, at, :] - top[pair, at, :])
        weights = pb[tile - pair, pair, at, :].astype(F32) * twice(factor)
        pb[tile - pair, pair, at, :] = weights.astype(BF16)
        dweight = dot(dox[pair, at, :], vx[tile * TILE:(tile + 1) * TILE, :], NT)
        ds = (weights * dweight).astype(BF16)
        dsb[tile % SLOTS, pair, at, :] = ds
        acc[pair, at, :] += dot(ds, kx[tile * TILE:(tile + 1) * TILE, :HEAD], NN)

    def pairs_of(tile):
        return [pair for pair in range(pairs) if pair <= tile < pair + TILES]

    def query_part(tile):
        for pair in pairs_of(tile):
            for chunk in range(chunks):
                score_gradient(tile, pair, slice(chunk * rows, (chunk + 1) * rows))

    def key_part(tile):
        dk = dv = None
        for pair in pairs_of(tile):
            more_k = dot(qt[pair], dsb[tile % SLOTS, pair], NN)
            more_v = dot(dt[pair], pb[tile - pair, pair], NN)
            dk = more_k if dk is None else dk + more_k
            dv = more_v if dv is None else dv + more_v
        return (dk * scale).T, dv.T

    def send_part(block):
        for tile in range(block * far, (block + 1) * far):
            at = slice((tile % far) * TILE, (tile % far + 1) * TILE)
            gradients = key_part(tile)
            sendb[block, at, :HEAD] = gradients[0].astype(BF16)
            sendb[block, at, HEAD:] = gradients[1].astype(BF16)
        part_copy(block).start()

    for block in range(REACH):
        for tile in range(block * far, (block + 1) * far):
            query_part(tile)
        if block < REACH - 1:
            send_part(block)

    def last_step(chunk, carry):
        at = chunk_rows(chunk)
        for tile in range(last, last + far):
            for pair in pairs_of(tile):
                score_gradient(tile, pair, at)
        for pair in range(pairs):
            gradient = acc[pair, at, :] * scale
            dqb[pair * TILE:(pair + 1) * TILE, columns(chunk * wide, wide)] = unstacked(gradient.astype(BF16))
        send_out(1, chunk)
        return carry

    lax.fori_loop(0, chunks, last_step, 0)
    send_part(REACH - 1)
    for tile in range(last, last + far):
        span = slice((tile - last) * TILE, (tile - last + 1) * TILE)
        akk[span, :], avv[span, :] = key_part(tile)
    own_dq = pltpu.make_async_copy(dqb.at[mine, :], grad_query.at[:, columns(me * group, group)], local.at[5])
    own_dq.start()

    for block in range(REACH):
        part_copy(block).wait_recv()
    for which, added_up in enumerate((akk, avv)):
        span = slice(which * HEAD, (which + 1) * HEAD)
        whole = added_up[...]
        for block in range(REACH):
            whole = whole + recvb[block, :, span].astype(F32)
        gb[which] = whole.astype(BF16)
    own_g = [
        pltpu.make_async_copy(gb.at[which, mine, :], ref.at[:, columns(me * HEAD, HEAD)], local.at[6 + which])
        for which, ref in enumerate((grad_key, grad_value))
    ]
    for which in range(2):
        for step in others:
            grad_copy(which, step).start()
        own_g[which].start()

    for which in range(2):
        for step in others:
            kv_copy(which, step).wait_send()
        for step in range(1, REACH + 1):
            window_copy(which, step).wait_send()
    for block in range(REACH):
        part_copy(block).wait_send()

    def drain(chunk, carry):
        for step in others:
            in_copy(0, chunk, step).wait_send()
            in_copy(1, chunk, step).wait_send()
            out_copy(0, chunk, step).wait()
            out_copy(1, chunk, step).wait()
        return carry

    lax.fori_loop(0, chunks, drain, 0)
    own_out.wait()
    own_dq.wait()
    for which in range(2):
        own_g[which].wait()
        for step in others:
            grad_copy(which, step).wait()


def per_device(query, key, value, cotangent, lengths):
    cp_size = lax.axis_size("cp")
    hp_size = lax.axis_size("hp")
    tokens = query.shape[0]
    heads = query.shape[1] // (HEAD * hp_size)
    shard = tokens * hp_size
    pairs = shard // TILE
    window = (REACH + 1) * shard
    chunks = heads // CHUNK_HEADS
    rows = TILE * CHUNK_HEADS
    total = heads * TILE
    anywhere = pl.BlockSpec(memory_space=pl.ANY)
    vmem = pltpu.VMEM
    dma = pltpu.SemaphoreType.DMA
    peers = hp_size - 1
    documents = lengths.shape[0]
    scratch = [
        vmem((1, documents), jnp.int32),
        vmem((shard, heads * HEAD), BF16),
        vmem((shard, heads * HEAD), BF16),
        vmem((window, 2 * HEAD), BF16),
        vmem((window, 2 * HEAD), BF16),
        vmem((shard, HEAD), BF16),
        vmem((TILES, pairs, total, TILE), BF16),
        vmem((SLOTS, pairs, total, TILE), BF16),
        vmem((shard, heads * HEAD), BF16),
        vmem((shard, heads * HEAD), BF16),
        vmem((pairs, total, HEAD), F32),
        vmem((pairs, total, HEAD), F32),
        vmem((pairs, total, HEAD), F32),
        vmem((REACH + 1, pairs, total, HEAD), F32),
        vmem((pairs, total, 2 * HEAD), BF16),
        vmem((pairs, HEAD, total), BF16),
        vmem((pairs, HEAD, total), BF16),
        vmem((shard, HEAD), F32),
        vmem((shard, HEAD), F32),
        vmem((REACH, shard, 2 * HEAD), BF16),
        vmem((REACH, shard, 2 * HEAD), BF16),
        vmem((2, shard, HEAD), BF16),
        dma((2, peers)), dma((2, peers)),
        dma((2, REACH)), dma((2, REACH)),
        dma((chunks, peers)), dma((chunks, peers)),
        dma((chunks, peers)), dma((chunks, peers)),
        dma((chunks, peers)), dma((chunks, peers)),
        dma((chunks, peers)), dma((chunks, peers)),
        dma((REACH,)), dma((REACH,)),
        dma((2, peers)), dma((2, peers)),
        dma((9,)),
    ]
    return pl.pallas_call(
        functools.partial(kernel, cp_size, hp_size, tokens, heads),
        out_shape=tuple(vmem(array.shape, BF16) for array in (query, query, key, value)),
        in_specs=[anywhere] * 5,
        out_specs=[pl.BlockSpec(memory_space=vmem)] * 4,
        scratch_shapes=scratch,
        compiler_params=pltpu.CompilerParams(
            collective_id=0, has_side_effects=True, vmem_limit_bytes=56 << 20
        ),
    )(query, key, value, cotangent, lengths.reshape(1, -1))


def solution(mesh):
    spec = P(("cp", "hp"), None)
    return jax.shard_map(
        per_device,
        mesh=mesh,
        in_specs=(spec, spec, spec, spec, P()),
        out_specs=(spec, spec, spec, spec),
        check_vma=False,
    )
```
